32 devices in a mesh: leaf: 2 (over y), grow: 4 (over z), gcol: 4 (over x, core).
Axes of the slice: x: 2, y: 2, z: 4, core: 2. Of those that a mesh axis runs over, the one named last changes fastest.
Arguments:
- right_leaf: float32 [2, 4, 4, 512, 256], P('leaf', 'grow', 'gcol'), may hold values from -6 to 6
- inverse_leaf: float32 [2, 4, 4, 512, 512], P('leaf', 'grow', 'gcol'), may hold values from -2 to 2
- lower_leaf: float32 [2, 4, 4, 512, 512], P('leaf', 'grow', 'gcol'), may hold values from -0.25 to 0.25
- present: int32 [2, 4, 4], P('leaf', 'grow', 'gcol'), may hold values 0 or 1
- right_middle: float32 [2, 4, 512, 256], P('leaf', 'grow', 'gcol'), may hold values from -6 to 6
- inverse_middle: float32 [2, 4, 512, 512], P('leaf', 'grow', 'gcol'), may hold values from -2 to 2
- upper_middle: float32 [2, 2, 4, 512, 512], P(None, 'leaf', 'grow', 'gcol'), may hold values from -0.09375 to 0.09375
- right_top: float32 [2, 512, 256], P(None, 'gcol'), may hold values from -6 to 6
- inverse_top: float32 [2, 512, 512], P(None, 'gcol'), may hold values from -2 to 2
- upper_top: float32 [1, 512, 512], P(None, 'gcol'), may hold values from -0.25 to 0.25
Outputs:
- solve_leaf: float32 [2, 4, 4, 512, 256], P('leaf', 'grow', 'gcol')
- solve_middle: float32 [2, 4, 512, 256], P('leaf', 'grow', 'gcol')
- solve_top: float32 [2, 512, 256], P(None, 'gcol')
The draws below stay inside these ranges and needn't reach their ends.
All inputs are finite; a program needn't handle non-finite values. No bound on the sum of `present` on one device may be relied on, other than what follows from the above.
Results may differ from the reference program's by a relative error of at most 0.00016.
Values sent between devices are 32-bit elements; how exact they have to be, the bound alone decides.
A program may use at most 64 MiB of HBM per device.

```python
import math
import jax
import jax.numpy as jnp
from jax import lax

BLK = 512
NRHS = 256
LEVELS = 2
LAYERS = 2
PROW = 4
PCOL = 4
PAIRS = 1


def dominant(key, shape):
    noise_key = jax.random.fold_in(key, 11)
    scale_key = jax.random.fold_in(key, 12)
    noise = jax.random.normal(noise_key, shape, jnp.float32) * (0.6 / math.sqrt(BLK))
    scales = jax.random.uniform(scale_key, shape[:-1] + (1,), jnp.float32, 0.7, 1.4)
    identity = jnp.eye(BLK, dtype=jnp.float32)
    return jnp.clip(identity * scales + noise, -2.0, 2.0)


def draw_inverse_leaf(key, part):
    return dominant(key, (LAYERS, PROW, PCOL, BLK, BLK))


def draw_inverse_middle(key, part):
    return dominant(key, (LAYERS, PROW, BLK, BLK))


def draw_inverse_top(key, part):
    return dominant(key, (LEVELS, BLK, BLK))


def plant(values, rng, low, top_value):
    extent = values.shape
    index_at = [jax.random.randint(jax.random.fold_in(rng, axis), (), 0, extent[axis]) for axis in range(len(extent))]
    values = values.at[tuple(index_at)].set(low)
    longest = extent.index(max(extent))
    index_at[longest] = (index_at[longest] + 1) % extent[longest]
    return values.at[tuple(index_at)].set(top_value)


def block_levels(own_key, shape, pieces, smallest, high):
    gain = 1.0
    for dim, blocks in pieces:
        steps = jax.random.uniform(jax.random.fold_in(jax.random.fold_in(own_key, 6), dim), (blocks,), jnp.float32, smallest / len(pieces), high / len(pieces))
        gain = gain * jnp.repeat(jnp.exp(steps), shape[dim] // blocks).reshape((-1,) + (1,) * (len(shape) - 1 - dim))
    return gain


def bell_draw(own_key, dims, width, bound, shards=(), kind=jnp.bfloat16):
    values = width * jax.random.normal(own_key, dims, jnp.float32)
    if shards:
        values = values * block_levels(own_key, dims, shards, -0.22, 0.18)
    return jnp.clip(values, -bound, bound).astype(kind)


def setup_inputs(seed: int = 0) -> dict:
    arg_keys = jax.random.split(jax.random.key(seed), 11)
    return {
        "right_leaf": bell_draw(arg_keys[0], (LAYERS, PROW, PCOL, BLK, NRHS), 1.0, 6.0, ((0, 2), (1, 4), (2, 4)), jnp.float32),
        "inverse_leaf": draw_inverse_leaf(jax.random.fold_in(arg_keys[10], 71), 0),
        "lower_leaf": bell_draw(arg_keys[2], (LAYERS, PROW, PCOL, BLK, BLK), BLK ** -0.5, 0.25, ((0, 2), (1, 4), (2, 4)), jnp.float32),
        "present": plant((jax.random.randint(arg_keys[3], (LAYERS, PROW, PCOL), 0, 4) < 3).astype(jnp.int32), jax.random.fold_in(arg_keys[3], 1), 0, 1),
        "right_middle": bell_draw(arg_keys[4], (LAYERS, PROW, BLK, NRHS), 1.0, 6.0, ((0, 2), (1, 4), (2, 4)), jnp.float32),
        "inverse_middle": draw_inverse_middle(jax.random.fold_in(arg_keys[10], 71), 0),
        "upper_middle": bell_draw(arg_keys[6], (LEVELS, LAYERS, PROW, BLK, BLK), (BLK * LAYERS * PROW) ** -0.5, 0.09375, ((1, 2), (2, 4), (3, 4)), jnp.float32),
        "right_top": bell_draw(arg_keys[7], (LEVELS, BLK, NRHS), 1.0, 6.0, ((1, 4),), jnp.float32),
        "inverse_top": draw_inverse_top(jax.random.fold_in(arg_keys[10], 71), 0),
        "upper_top": bell_draw(arg_keys[9], (PAIRS, BLK, BLK), BLK ** -0.5, 0.25, ((1, 4),), jnp.float32),
    }


PRECISE = lax.Precision.HIGHEST


def product(formula, first_arg, second_arg):
    return jnp.einsum(formula, first_arg, second_arg, precision=PRECISE, preferred_element_type=jnp.float32)


def pair_index(upper_level, lower_level):
    return upper_level * (upper_level - 1) // 2 + lower_level


def reference(right_leaf, inverse_leaf, lower_leaf, present, right_middle, inverse_middle, upper_middle, right_top, inverse_top, upper_top):
    present_scale = present.astype(jnp.float32)[..., None, None]
    leaf_fwd = product('lrcij,lrcjn->lrcin', inverse_leaf, right_leaf)
    middle_sum = product('lrcij,lrcjn->lrin', lower_leaf, leaf_fwd * present_scale)
    middle_fwd = product('lrij,lrjn->lrin', inverse_middle, right_middle - middle_sum)
    top_sum = product('klrji,lrjn->kin', upper_middle, middle_fwd)
    top_fwd = []
    for upper_level in range(LEVELS):
        residual = right_top[upper_level] - top_sum[upper_level]
        for lower_level in range(upper_level):
            residual = residual - product('ji,jn->in', upper_top[pair_index(upper_level, lower_level)], top_fwd[lower_level])
        top_fwd.append(product('ij,jn->in', inverse_top[upper_level], residual))
    top_back = [None] * LEVELS
    for upper_level in reversed(range(LEVELS)):
        residual = top_fwd[upper_level]
        for higher_level in range(upper_level + 1, LEVELS):
            residual = residual - product('ij,jn->in', upper_top[pair_index(higher_level, upper_level)], top_back[higher_level])
        top_back[upper_level] = product('ji,jn->in', inverse_top[upper_level], residual)
    solve_top = jnp.stack(top_back)
    middle_res = middle_fwd - product('klrij,kjn->lrin', upper_middle, solve_top)
    solve_middle = product('lrji,lrjn->lrin', inverse_middle, middle_res)
    leaf_res = leaf_fwd - product('lrcji,lrjn->lrcin', lower_leaf, solve_middle) * present_scale
    solve_leaf = product('lrcji,lrcjn->lrcin', inverse_leaf, leaf_res)
    return solve_leaf, solve_middle, solve_top
```

```python
import functools

import jax
import jax.numpy as jnp
from jax import lax
from jax.experimental import pallas as pl
from jax.experimental.pallas import tpu as pltpu
from jax.sharding import PartitionSpec as P

AXES = ("gcol", "leaf", "grow")
NN = ((1,), (0,))
NT = ((1,), (1,))


def pair_index(upper_level, lower_level):
    return upper_level * (upper_level - 1) // 2 + lower_level


def split(value):
    high = value.astype(jnp.bfloat16)
    low = (value - high.astype(jnp.float32)).astype(jnp.bfloat16)
    return high, low


def mul(left, right, dims=NN):
    def dot(a, b):
        return lax.dot_general(a, b, (dims, ((), ())), preferred_element_type=jnp.float32)

    return dot(left[0], right[0]) + (dot(left[0], right[1]) + dot(left[1], right[0]))


class Plan:
    def __init__(self, sizes, levels, block, columns):
        self.sizes, self.levels, self.block, self.columns = sizes, levels, block, columns
        self.n = sizes["gcol"]
        self.gbits = [("gcol", t) for t in range(self.n.bit_length() - 1)]
        others = [(a, t) for a in AXES[1:] for t in range(sizes[a].bit_length() - 1)]
        bits = self.gbits + others
        count = 0
        while count < len(bits) and columns >> (count + 1) >= 8:
            count += 1
        count = max(count, len(self.gbits))
        self.halved, self.rest = bits[:count], bits[count:]
        self.chunk = columns >> count
        first = self.gbits[:1]
        self.orders = [
            self.halved,
            first
            + [b for b in self.halved if b[0] == "leaf"]
            + [b for b in self.halved if b[0] == "gcol" and b not in first]
            + [b for b in self.halved if b[0] == "grow"],
        ]
        self.all_bits = bits

    def order(self, level):
        return self.orders[level % 2]


def kernel(
    plan,
    right_leaf,
    inverse_leaf,
    lower_leaf,
    present,
    right_middle,
    inverse_middle,
    upper_middle,
    right_top,
    inverse_top,
    upper_top,
    solve_leaf,
    solve_middle,
    solve_top,
    *scratch,
):
    names = [name for name, _ in scratch_list(plan)]
    s = dict(zip(names, scratch))
    send, recv = s["send"], s["recv"]
    n, levels, block, columns, chunk = plan.n, plan.levels, plan.block, plan.columns, plan.chunk
    share = block // n
    nbits = len(plan.gbits)
    place = {axis: lax.axis_index(axis) for axis in AXES}
    me = place["gcol"]
    counter = [0]

    def bit_of(bit):
        return (place[bit[0]] // 2 ** bit[1]) % 2

    def partner(bit):
        return {bit[0]: place[bit[0]] + (1 - 2 * bit_of(bit)) * 2 ** bit[1]}

    def ship(source, target, bit):
        slot = counter[0]
        counter[0] += 1
        copy = pltpu.make_async_remote_copy(
            src_ref=source,
            dst_ref=target,
            send_sem=send.at[slot],
            recv_sem=recv.at[slot],
            device_id=partner(bit),
            device_id_type=pl.DeviceIdType.MESH,
        )
        copy.start()
        return copy

    barrier = pltpu.get_barrier_semaphore()
    for bit in plan.all_bits:
        pl.semaphore_signal(
            barrier, inc=1, device_id=partner(bit), device_id_type=pl.DeviceIdType.MESH
        )

    kept = present[0, 0, 0].astype(jnp.float32)
    leaf_fwd = mul(split(inverse_leaf[0, 0, 0]), split(right_leaf[0, 0, 0]))
    s["leaf_fwd"][...] = leaf_fwd
    part = mul(split(lower_leaf[0, 0, 0]), split(leaf_fwd)) * kept
    s["mid"][...] = part.reshape(n, share, columns)
    pl.semaphore_wait(barrier, len(plan.all_bits))

    def scatter_sum(blocks, landing, idle=None):
        at = 0
        for t, bit in enumerate(plan.gbits):
            low = me % 2**t
            count = n >> (t + 1)
            theirs = low + (1 - bit_of(bit)) * 2**t
            mine = low + bit_of(bit) * 2**t
            copies = [
                ship(blocks.at[theirs + j * 2 ** (t + 1)], landing.at[at + j], bit)
                for j in range(count)
            ]
            if idle is not None:
                idle(t)
            for j, copy in enumerate(copies):
                copy.wait()
                where = mine + j * 2 ** (t + 1)
                blocks[where] = blocks[where] + landing[at + j]
            at += count

    def gather(blocks, idle=None):
        for t in reversed(range(nbits)):
            low = me % 2 ** (t + 1)
            copies = [
                ship(*(blocks.at[low + j * 2 ** (t + 1)],) * 2, plan.gbits[t])
                for j in range(n >> (t + 1))
            ]
            if idle is not None:
                idle(t)
            for copy in copies:
                copy.wait()

    def fill_transposes(t):
        if t == nbits - 1:
            high, low = split(inverse_leaf[0, 0, 0].T)
            s["inv_high"][...] = high
            s["inv_low"][...] = low

    def fill_lower(t):
        if t == nbits - 1:
            high, low = split(lower_leaf[0, 0, 0].T)
            s["low_high"][...] = high
            s["low_low"][...] = low

    scatter_sum(s["mid"], s["mid_land"], fill_transposes)
    s["mid_full"][me] = right_middle[0, 0] - s["mid"][me]
    gather(s["mid_full"], fill_lower)
    inv_mid = inverse_middle[0, 0]
    middle_fwd = mul(split(inv_mid), split(s["mid_full"][...].reshape(block, columns)))

    lead = ((place["leaf"] + place["grow"]) == 0).astype(jnp.float32)
    fwd_turned = split(middle_fwd.T)
    bits_shape = (2,) * len(plan.halved)
    for level in range(levels):
        turned = mul(fwd_turned, split(upper_middle[level, 0, 0]))
        right = right_top[level].T * lead
        placed = jnp.concatenate(
            [right * (me == c).astype(jnp.float32) for c in range(n)], axis=1
        )
        s[f"top{level}"][...] = (placed - turned).reshape(bits_shape + (chunk, block))

    def index(done, bit=None, flip=False):
        where = []
        for b in plan.halved:
            if b in done:
                where.append(bit_of(b))
            elif b == bit:
                where.append(1 - bit_of(b) if flip else bit_of(b))
            else:
                where.append(slice(None))
        return tuple(where)

    for step in range(len(plan.halved)):
        copies = []
        for level in range(levels):
            order = plan.order(level)
            top = s[f"top{level}"]
            there = index(order[:step], order[step], True)
            copies.append(ship(top.at[there], s[f"land{level}_{step}"], order[step]))
        for level in range(levels):
            order = plan.order(level)
            top = s[f"top{level}"]
            here = index(order[: step + 1])
            copies[level].wait()
            top[here] = top[here] + s[f"land{level}_{step}"][...]
    own = index(plan.halved)
    for step, bit in enumerate(plan.rest):
        copies = [
            ship(s[f"top{level}"].at[own], s["rest"].at[step, level], bit)
            for level in range(levels)
        ]
        for level in range(levels):
            copies[level].wait()
            s[f"top{level}"][own] = s[f"top{level}"][own] + s["rest"][step, level]

    for level in range(levels):
        s["group"][me, level] = s[f"top{level}"][own]
    gather(s["group"])

    rows = n * chunk
    uses = [0]

    def total(value):
        for bit in plan.gbits:
            slot = uses[0]
            uses[0] += 1
            s["tot_out"][slot] = value
            ship(s["tot_out"].at[slot], s["tot_in"].at[slot], bit).wait()
            value = value + s["tot_in"][slot]
        return value

    inverses = [split(inverse_top[level]) for level in range(levels)]
    top_fwd = []
    for level in range(levels):
        residual = s["group"][:, level].reshape(rows, block)
        if level > 0:
            terms = 0.0
            for lower in range(level):
                terms = terms + mul(
                    split(top_fwd[lower]), split(upper_top[pair_index(level, lower)])
                )
            residual = residual - total(terms)
        top_fwd.append(mul(split(residual), inverses[level], NT))
    top_back = [None] * levels
    for level in reversed(range(levels)):
        residual = top_fwd[level]
        for higher in range(level + 1, levels):
            residual = residual - mul(
                split(top_back[higher]), split(upper_top[pair_index(higher, level)]), NT
            )
        top_back[level] = total(mul(split(residual), inverses[level]))
        s["answer"][level] = top_back[level].reshape(n, chunk, block)

    for step in reversed(range(len(plan.halved))):
        copies = []
        for level in range(levels):
            order = plan.order(level)
            mine = s[f"back{level}"]
            held = index(order[: step + 1])
            if step == len(plan.halved) - 1:
                mine[held] = s["answer"][level, me]
            copies.append(ship(mine.at[held], mine.at[held], order[step]))
        for copy in copies:
            copy.wait()

    residual = middle_fwd
    for level in range(levels):
        turned = s[f"back{level}"][...].reshape(columns, block)
        residual = residual - mul(split(upper_middle[level, 0, 0]), split(turned), NT)
    s["mid2"][...] = mul(split(inv_mid.T), split(residual)).reshape(n, share, columns)

    def fill_top(t):
        if t == nbits - 1:
            for level in range(levels):
                s["top_rows"][level] = s[f"back{level}"][...].reshape(columns, block).T
                start = pl.multiple_of(me * share, share)
                solve_top[level] = s["top_rows"][level, pl.ds(start, share), :]

    scatter_sum(s["mid2"], s["mid2_land"], fill_top)
    solve_middle[0, 0] = s["mid2"][me]
    s["mid2_full"][me] = s["mid2"][me]
    gather(s["mid2_full"])
    middle = split(s["mid2_full"][...].reshape(block, columns))
    leaf_res = s["leaf_fwd"][...] - kept * mul((s["low_high"][...], s["low_low"][...]), middle)
    solve_leaf[0, 0, 0] = mul((s["inv_high"][...], s["inv_low"][...]), split(leaf_res))


def scratch_list(plan):
    n, levels, block, columns, chunk = plan.n, plan.levels, plan.block, plan.columns, plan.chunk
    share = block // n
    f32, b16 = jnp.float32, jnp.bfloat16
    nh, nbits = len(plan.halved), len(plan.gbits)
    alls = nbits * (2 * levels)
    slots = 4 * (n - 1) + (2 * nh + len(plan.rest)) * levels + (n - 1) + alls
    out = [
        ("send", pltpu.SemaphoreType.DMA((slots,))),
        ("recv", pltpu.SemaphoreType.DMA((slots,))),
        ("leaf_fwd", pltpu.VMEM((block, columns), f32)),
        ("inv_high", pltpu.VMEM((block, block), b16)),
        ("inv_low", pltpu.VMEM((block, block), b16)),
        ("low_high", pltpu.VMEM((block, block), b16)),
        ("low_low", pltpu.VMEM((block, block), b16)),
        ("mid", pltpu.VMEM((n, share, columns), f32)),
        ("mid_land", pltpu.VMEM((n - 1, share, columns), f32)),
        ("mid_full", pltpu.VMEM((n, share, columns), f32)),
        ("mid2", pltpu.VMEM((n, share, columns), f32)),
        ("mid2_full", pltpu.VMEM((n, share, columns), f32)),
        ("mid2_land", pltpu.VMEM((n - 1, share, columns), f32)),
        ("group", pltpu.VMEM((n, levels, chunk, block), f32)),
        ("answer", pltpu.VMEM((levels, n, chunk, block), f32)),
        ("tot_out", pltpu.VMEM((alls, n * chunk, block), f32)),
        ("tot_in", pltpu.VMEM((alls, n * chunk, block), f32)),
        ("top_rows", pltpu.VMEM((levels, block, columns), f32)),
    ]
    if plan.rest:
        out.append(("rest", pltpu.VMEM((len(plan.rest), levels, chunk, block), f32)))
    for level in range(levels):
        out.append((f"top{level}", pltpu.VMEM((2,) * nh + (chunk, block), f32)))
        out.append((f"back{level}", pltpu.VMEM((2,) * nh + (chunk, block), f32)))
        for step in range(nh):
            shape = (2,) * (nh - step - 1) + (chunk, block)
            out.append((f"land{level}_{step}", pltpu.VMEM(shape, f32)))
    return out


def local(sizes, *args):
    right_leaf, right_middle, right_top = args[0], args[4], args[7]
    block, columns = right_leaf.shape[-2:]
    plan = Plan(sizes, right_top.shape[0], block, columns)
    vmem = pl.BlockSpec(memory_space=pltpu.VMEM)
    in_specs = [vmem] * len(args)
    in_specs[3] = pl.BlockSpec(memory_space=pltpu.SMEM)
    return pl.pallas_call(
        functools.partial(kernel, plan),
        out_shape=(
            jax.ShapeDtypeStruct(right_leaf.shape, jnp.float32),
            jax.ShapeDtypeStruct(right_middle.shape, jnp.float32),
            jax.ShapeDtypeStruct(right_top.shape, jnp.float32),
        ),
        in_specs=in_specs,
        out_specs=(vmem,) * 3,
        scratch_shapes=[shape for _, shape in scratch_list(plan)],
        compiler_params=pltpu.CompilerParams(
            collective_id=0, has_side_effects=True, vmem_limit_bytes=56 * 2**20
        ),
    )(*args)


def solution(mesh):
    in_specs = (
        P("leaf", "grow", "gcol", None, None),
        P("leaf", "grow", "gcol", None, None),
        P("leaf", "grow", "gcol", None, None),
        P("leaf", "grow", "gcol"),
        P("leaf", "grow", "gcol", None),
        P("leaf", "grow", "gcol", None),
        P(None, "leaf", "grow", "gcol", None),
        P(None, "gcol", None),
        P(None, "gcol", None),
        P(None, "gcol", None),
    )
    out_specs = (
        P("leaf", "grow", "gcol", None, None),
        P("leaf", "grow", "gcol", None),
        P(None, "gcol", None),
    )
    sizes = {axis: mesh.shape[axis] for axis in AXES}
    return jax.shard_map(
        functools.partial(local, sizes),
        mesh=mesh,
        in_specs=in_specs,
        out_specs=out_specs,
        check_vma=False,
    )
```

```python
import functools

import jax
import jax.numpy as jnp
from jax import lax
from jax.experimental import pallas as pl
from jax.experimental.pallas import tpu as pltpu
from jax.sharding import PartitionSpec as P

PARTS = 2
AXES = ("gcol", "leaf", "grow")
NN = ((1,), (0,))
NT = ((1,), (1,))


def pair_index(upper_level, lower_level):
    return upper_level * (upper_level - 1) // 2 + lower_level


def split(value):
    high = value.astype(jnp.bfloat16)
    low = (value - high.astype(jnp.float32)).astype(jnp.bfloat16)
    return high, low


def mul(left, right, dims=NN):
    def dot(a, b):
        return lax.dot_general(a, b, (dims, ((), ())), preferred_element_type=jnp.float32)

    return dot(left[0], right[0]) + (dot(left[0], right[1]) + dot(left[1], right[0]))


class Plan:
    def __init__(self, sizes, levels, block, columns):
        self.sizes, self.levels, self.block = sizes, levels, block
        self.parts = PARTS
        self.columns, self.width = columns, columns // PARTS
        self.n = sizes["gcol"]
        self.gbits = [("gcol", t) for t in range(self.n.bit_length() - 1)]
        others = [(a, t) for a in AXES[1:] for t in range(sizes[a].bit_length() - 1)]
        self.bits = self.gbits + others
        count = 0
        while count < len(self.bits) and self.width >> (count + 1) >= 8:
            count += 1
        self.halved, self.rest = self.bits[:count], self.bits[count:]
        self.chunk = self.width >> count
        first = self.gbits[:1]
        self.orders = [
            self.halved,
            first
            + [b for b in self.halved if b[0] == "leaf"]
            + [b for b in self.halved if b[0] == "gcol" and b not in first]
            + [b for b in self.halved if b[0] == "grow"],
        ]
        self.mats = levels + levels * (levels - 1) // 2

    def order(self, level):
        return self.orders[level % 2]

    def slots(self):
        n, nx = self.n, self.n // 2
        middle = 4 * (n - 1)
        top = (2 * len(self.halved) + len(self.rest)) * self.levels
        spread = self.mats * (1 + 4 * (nx - 1))
        return self.parts * (middle + top) + spread


def kernel(
    plan,
    right_leaf,
    inverse_leaf,
    lower_leaf,
    present,
    right_middle,
    inverse_middle,
    upper_middle,
    right_top,
    inverse_top,
    upper_top,
    solve_leaf,
    solve_middle,
    solve_top,
    *scratch,
):
    names = [name for name, _ in scratch_list(plan)]
    s = dict(zip(names, scratch))
    send, recv = s["send"], s["recv"]
    n, levels, block, chunk, width = plan.n, plan.levels, plan.block, plan.chunk, plan.width
    share = block // n
    nbits = len(plan.gbits)
    place = {axis: lax.axis_index(axis) for axis in AXES}
    me = place["gcol"]
    counter = [0]

    def bit_of(bit):
        return (place[bit[0]] // 2 ** bit[1]) % 2

    def partner(bit):
        return {bit[0]: place[bit[0]] + (1 - 2 * bit_of(bit)) * 2 ** bit[1]}

    def ship(source, target, where):
        slot = counter[0]
        counter[0] += 1
        copy = pltpu.make_async_remote_copy(
            src_ref=source,
            dst_ref=target,
            send_sem=send.at[slot],
            recv_sem=recv.at[slot],
            device_id=where,
            device_id_type=pl.DeviceIdType.MESH,
        )
        copy.start()
        return copy

    nx = n // 2
    core, row_x = me % 2, me // 2
    half_rows = share // 2
    mate, opposite = partner(("gcol", 0)), partner(("leaf", 0))
    half = bit_of(("leaf", 0))
    tops = s["tops"]
    offsets = range(1, nx)

    barrier = pltpu.get_barrier_semaphore()
    far = [{"gcol": (row_x + d) % nx * 2 + core} for d in offsets]
    greeted = [partner(bit) for bit in plan.bits if bit[0] != "gcol" or bit[1] == 0] + far
    for device in greeted:
        pl.semaphore_signal(
            barrier, inc=1, device_id=device, device_id_type=pl.DeviceIdType.MESH
        )
    for level in range(levels):
        tops[level, me] = inverse_top[level].reshape(2, half_rows, block)
    for pair in range(plan.mats - levels):
        tops[levels + pair, me] = upper_top[pair].reshape(2, half_rows, block)
    pl.semaphore_wait(barrier, len(greeted))

    first, second = list(range(levels)), list(range(levels, plan.mats))
    across, over, mated = {}, {}, []

    def came_from(d):
        return (row_x - d + nx) % nx * 2 + core

    def send_across(mats):
        for m in mats:
            mine = tops.at[m, me, half]
            across[m] = [ship(mine, mine, device) for device in far]

    def send_over(mats):
        for m in mats:
            over[m] = []
            for d, copy in zip(offsets, across[m]):
                copy.wait()
                piece = tops.at[m, came_from(d), half]
                over[m].append(ship(piece, piece, opposite))
                mated.append(ship(piece, piece, mate))

    def end_over(mats):
        for m in mats:
            for d, copy in zip(offsets, over[m]):
                copy.wait()
                piece = tops.at[m, came_from(d), 1 - half]
                mated.append(ship(piece, piece, mate))

    send_across(first)
    for m in first + second:
        mated.append(ship(tops.at[m, me], tops.at[m, me], mate))
    done = set()

    def once(name, act):
        if name not in done:
            done.add(name)
            act()

    kept = present[0, 0, 0].astype(jnp.float32)
    leaf_fwd = mul(split(inverse_leaf[0, 0, 0]), split(right_leaf[0, 0, 0]))
    s["leaf_fwd"][...] = leaf_fwd
    lower_pair = split(lower_leaf[0, 0, 0])
    inv_mid = inverse_middle[0, 0]
    lead = ((place["leaf"] + place["grow"]) == 0).astype(jnp.float32)
    bits_shape = (2,) * len(plan.halved)

    def fill_inverse():
        high, low = split(inverse_leaf[0, 0, 0].T)
        s["inv_high"][...] = high
        s["inv_low"][...] = low

    def fill_lower():
        high, low = split(lower_leaf[0, 0, 0].T)
        s["low_high"][...] = high
        s["low_low"][...] = low

    def split_tops():
        for m in range(plan.mats):
            high, low = split(tops[m].reshape(block, block))
            s["top_high"][m] = high
            s["top_low"][m] = low

    def narrow(value, m, dims):
        rest = value - value.astype(jnp.bfloat16).astype(jnp.float32)
        both = jnp.concatenate([value, rest], axis=0).astype(jnp.bfloat16)
        high, low = s["top_high"][m], s["top_low"][m]

        def dot(a, b):
            return lax.dot_general(a, b, (dims, ((), ())), preferred_element_type=jnp.float32)

        wide = dot(both, high)
        return wide[:chunk] + (wide[chunk:] + dot(both, low)[:chunk])

    def index(known, bit=None, flip=False):
        where = []
        for b in plan.halved:
            if b in known:
                where.append(bit_of(b))
            elif b == bit:
                where.append(1 - bit_of(b) if flip else bit_of(b))
            else:
                where.append(slice(None))
        return tuple(where)

    def scatter_sum(blocks, landing):
        at = 0
        for t, bit in enumerate(plan.gbits):
            low = me % 2**t
            count = n >> (t + 1)
            theirs = low + (1 - bit_of(bit)) * 2**t
            mine = low + bit_of(bit) * 2**t
            copies = [
                ship(blocks.at[theirs + j * 2 ** (t + 1)], landing.at[at + j], partner(bit))
                for j in range(count)
            ]
            yield
            for j, copy in enumerate(copies):
                copy.wait()
                where = mine + j * 2 ** (t + 1)
                blocks[where] = blocks[where] + landing[at + j]
            at += count

    def gather(blocks):
        for t in reversed(range(nbits)):
            low = me % 2 ** (t + 1)
            copies = [
                ship(*(blocks.at[low + j * 2 ** (t + 1)],) * 2, partner(plan.gbits[t]))
                for j in range(n >> (t + 1))
            ]
            yield
            for copy in copies:
                copy.wait()

    def pipeline(p):
        cols = slice(p * width, (p + 1) * width)
        own = index(plan.halved)
        mid, mid_full = s["mid"].at[p], s["mid_full"].at[p]
        part = mul(lower_pair, split(s["leaf_fwd"][:, cols])) * kept
        mid[...] = part.reshape(n, share, width)
        steps = scatter_sum(mid, s["mid_land"].at[p])
        next(steps)
        once("inverse", fill_inverse)
        yield
        for _ in steps:
            once("lower", fill_lower)
            yield
        mid_full[me] = right_middle[0, 0, :, cols] - mid[me]
        steps = gather(mid_full)
        next(steps)
        once("over", lambda: send_over(first))
        yield
        yield from steps
        middle_fwd = mul(split(inv_mid), split(mid_full[...].reshape(block, width)))
        s["middle_fwd"][p] = middle_fwd

        fwd_turned = split(middle_fwd.T)
        for level in range(levels):
            turned = mul(fwd_turned, split(upper_middle[level, 0, 0]))
            right = right_top[level, :, cols].T * lead
            placed = jnp.concatenate(
                [right * (me == c).astype(jnp.float32) for c in range(n)], axis=1
            )
            s[f"top{p}_{level}"][...] = (placed - turned).reshape(bits_shape + (chunk, block))
        for step in range(len(plan.halved)):
            copies = []
            for level in range(levels):
                order = plan.order(level)
                there = index(order[:step], order[step], True)
                copies.append(
                    ship(
                        s[f"top{p}_{level}"].at[there],
                        s[f"land{p}_{level}_{step}"],
                        partner(order[step]),
                    )
                )
            if step == 0:
                once("across", lambda: send_across(second))
            if step == 1:
                once("end", lambda: end_over(first))
            if step == 3:
                once("over2", lambda: send_over(second))
            yield
            for level in range(levels):
                here = index(plan.order(level)[: step + 1])
                top = s[f"top{p}_{level}"]
                copies[level].wait()
                top[here] = top[here] + s[f"land{p}_{level}_{step}"][...]
        for step, bit in enumerate(plan.rest):
            copies = [
                ship(
                    s[f"top{p}_{level}"].at[own],
                    s[f"rest{p}"].at[step, level],
                    partner(bit),
                )
                for level in range(levels)
            ]
            once("over2", lambda: send_over(second))
            once("end2", lambda: end_over(second))
            yield
            for level in range(levels):
                top = s[f"top{p}_{level}"]
                copies[level].wait()
                top[own] = top[own] + s[f"rest{p}"][step, level]

        def finish_tops():
            once("over2", lambda: send_over(second))
            once("end2", lambda: end_over(second))
            for copy in mated:
                copy.wait()
            split_tops()

        once("tops", finish_tops)
        top_fwd = []
        for level in range(levels):
            residual = s[f"top{p}_{level}"][own]
            for lower in range(level):
                m = levels + pair_index(level, lower)
                residual = residual - narrow(top_fwd[lower], m, NN)
            top_fwd.append(narrow(residual, level, NT))
        top_back = [None] * levels
        for level in reversed(range(levels)):
            residual = top_fwd[level]
            for higher in range(level + 1, levels):
                m = levels + pair_index(higher, level)
                residual = residual - narrow(top_back[higher], m, NT)
            top_back[level] = narrow(residual, level, NN)
            s[f"back{p}_{level}"][own] = top_back[level]
        for step in reversed(range(len(plan.halved))):
            copies = []
            for level in range(levels):
                order = plan.order(level)
                held = s[f"back{p}_{level}"].at[index(order[: step + 1])]
                copies.append(ship(held, held, partner(order[step])))
            yield
            for copy in copies:
                copy.wait()

        residual = s["middle_fwd"][p]
        for level in range(levels):
            turned = s[f"back{p}_{level}"][...].reshape(width, block)
            residual = residual - mul(split(upper_middle[level, 0, 0]), split(turned), NT)
        mid2, mid2_full = s["mid2"].at[p], s["mid2_full"].at[p]
        mid2[...] = mul(split(inv_mid.T), split(residual)).reshape(n, share, width)
        steps = scatter_sum(mid2, s["mid2_land"].at[p])
        next(steps)
        for level in range(levels):
            rows = s["top_rows"].at[level]
            rows[...] = s[f"back{p}_{level}"][...].reshape(width, block).T
            solve_top[level, :, cols] = rows[pl.ds(pl.multiple_of(me * share, share), share), :]
        yield
        yield from steps
        solve_middle[0, 0, :, cols] = mid2[me]
        mid2_full[me] = mid2[me]
        yield from gather(mid2_full)
        middle = split(mid2_full[...].reshape(block, width))
        leaf_res = s["leaf_fwd"][:, cols] - kept * mul(
            (s["low_high"][...], s["low_low"][...]), middle
        )
        solve_leaf[0, 0, 0, :, cols] = mul((s["inv_high"][...], s["inv_low"][...]), split(leaf_res))

    running = [pipeline(p) for p in range(plan.parts)]
    while running:
        running = [steps for steps in running if next(steps, StopIteration) is not StopIteration]


def scratch_list(plan):
    n, levels, block, width, chunk = plan.n, plan.levels, plan.block, plan.width, plan.chunk
    share, parts = block // n, plan.parts
    f32, b16 = jnp.float32, jnp.bfloat16
    nh, slots = len(plan.halved), plan.slots()
    out = [
        ("send", pltpu.SemaphoreType.DMA((slots,))),
        ("recv", pltpu.SemaphoreType.DMA((slots,))),
        ("leaf_fwd", pltpu.VMEM((block, plan.columns), f32)),
        ("inv_high", pltpu.VMEM((block, block), b16)),
        ("inv_low", pltpu.VMEM((block, block), b16)),
        ("low_high", pltpu.VMEM((block, block), b16)),
        ("low_low", pltpu.VMEM((block, block), b16)),
        ("mid", pltpu.VMEM((parts, n, share, width), f32)),
        ("mid_land", pltpu.VMEM((parts, n - 1, share, width), f32)),
        ("mid_full", pltpu.VMEM((parts, n, share, width), f32)),
        ("middle_fwd", pltpu.VMEM((parts, share, width), f32)),
        ("mid2", pltpu.VMEM((parts, n, share, width), f32)),
        ("mid2_full", pltpu.VMEM((parts, n, share, width), f32)),
        ("mid2_land", pltpu.VMEM((parts, n - 1, share, width), f32)),
        ("tops", pltpu.VMEM((plan.mats, n, 2, share // 2, block), f32)),
        ("top_high", pltpu.VMEM((plan.mats, block, block), b16)),
        ("top_low", pltpu.VMEM((plan.mats, block, block), b16)),
        ("top_rows", pltpu.VMEM((levels, block, width), f32)),
    ]
    for p in range(parts):
        if plan.rest:
            out.append((f"rest{p}", pltpu.VMEM((len(plan.rest), levels, chunk, block), f32)))
        for level in range(levels):
            out.append((f"top{p}_{level}", pltpu.VMEM((2,) * nh + (chunk, block), f32)))
            out.append((f"back{p}_{level}", pltpu.VMEM((2,) * nh + (chunk, block), f32)))
            for step in range(nh):
                shape = (2,) * (nh - step - 1) + (chunk, block)
                out.append((f"land{p}_{level}_{step}", pltpu.VMEM(shape, f32)))
    return out


def copy_out(*refs):
    count = len(refs) // 2
    sems = refs[-1]
    copies = [
        pltpu.make_async_copy(refs[i], refs[count + i], sems.at[i]) for i in range(count)
    ]
    for copy in copies:
        copy.start()
    for copy in copies:
        copy.wait()


def local(sizes, *args):
    right_leaf, right_middle, right_top = args[0], args[4], args[7]
    block, columns = right_leaf.shape[-2:]
    plan = Plan(sizes, right_top.shape[0], block, columns)
    vmem = pl.BlockSpec(memory_space=pltpu.VMEM)
    in_specs = [vmem] * len(args)
    in_specs[3] = pl.BlockSpec(memory_space=pltpu.SMEM)
    solved = pl.pallas_call(
        functools.partial(kernel, plan),
        out_shape=(
            jax.ShapeDtypeStruct(right_leaf.shape, jnp.float32),
            jax.ShapeDtypeStruct(right_middle.shape, jnp.float32),
            jax.ShapeDtypeStruct(right_top.shape, jnp.float32),
        ),
        in_specs=in_specs,
        out_specs=(vmem,) * 3,
        scratch_shapes=[shape for _, shape in scratch_list(plan)],
        compiler_params=pltpu.CompilerParams(
            collective_id=0, has_side_effects=True, vmem_limit_bytes=56 * 2**20
        ),
    )(*args)
    anywhere = pl.BlockSpec(memory_space=pl.ANY)
    return pl.pallas_call(
        copy_out,
        out_shape=tuple(jax.ShapeDtypeStruct(x.shape, x.dtype) for x in solved),
        in_specs=[anywhere] * len(solved),
        out_specs=(anywhere,) * len(solved),
        scratch_shapes=[pltpu.SemaphoreType.DMA((len(solved),))],
    )(*solved)


def solution(mesh):
    in_specs = (
        P("leaf", "grow", "gcol", None, None),
        P("leaf", "grow", "gcol", None, None),
        P("leaf", "grow", "gcol", None, None),
        P("leaf", "grow", "gcol"),
        P("leaf", "grow", "gcol", None),
        P("leaf", "grow", "gcol", None),
        P(None, "leaf", "grow", "gcol", None),
        P(None, "gcol", None),
        P(None, "gcol", None),
        P(None, "gcol", None),
    )
    out_specs = (
        P("leaf", "grow", "gcol", None, None),
        P("leaf", "grow", "gcol", None),
        P(None, "gcol", None),
    )
    sizes = {axis: mesh.shape[axis] for axis in AXES}
    return jax.shard_map(
        functools.partial(local, sizes),
        mesh=mesh,
        in_specs=in_specs,
        out_specs=out_specs,
        check_vma=False,
    )
```

```python
import functools

import jax
import jax.numpy as jnp
from jax import lax
from jax.experimental import pallas as pl
from jax.experimental.pallas import tpu as pltpu
from jax.sharding import PartitionSpec as P

PARTS = 2
AXES = ("gcol", "leaf", "grow")
NN = ((1,), (0,))
NT = ((1,), (1,))


def pair_index(upper_level, lower_level):
    return upper_level * (upper_level - 1) // 2 + lower_level


def split(value):
    high = value.astype(jnp.bfloat16)
    low = (value - high.astype(jnp.float32)).astype(jnp.bfloat16)
    return high, low


def mul(left, right, dims=NN):
    def dot(a, b):
        return lax.dot_general(a, b, (dims, ((), ())), preferred_element_type=jnp.float32)

    return dot(left[0], right[0]) + (dot(left[0], right[1]) + dot(left[1], right[0]))


class Plan:
    def __init__(self, sizes, levels, block, columns):
        self.sizes, self.levels, self.block = sizes, levels, block
        self.parts = PARTS
        self.columns, self.width = columns, columns // PARTS
        self.n = sizes["gcol"]
        self.gbits = [("gcol", t) for t in range(self.n.bit_length() - 1)]
        others = [(a, t) for a in AXES[1:] for t in range(sizes[a].bit_length() - 1)]
        self.bits = self.gbits + others
        count = 0
        while count < len(self.bits) and self.width >> (count + 1) >= 8:
            count += 1
        self.halved, self.rest = self.bits[:count], self.bits[count:]
        self.chunk = self.width >> count
        first = self.gbits[:1]
        self.orders = [
            self.halved,
            first
            + [b for b in self.halved if b[0] == "leaf"]
            + [b for b in self.halved if b[0] == "gcol" and b not in first]
            + [b for b in self.halved if b[0] == "grow"],
        ]
        self.mats = levels + levels * (levels - 1) // 2

    def order(self, level):
        return self.orders[level % 2]

    def slots(self):
        n, nx = self.n, self.n // 2
        middle = 4 * (n - 1)
        top = (2 * len(self.halved) + len(self.rest)) * self.levels
        spread = self.mats * (1 + 5 * (nx - 1))
        return self.parts * (middle + top) + spread


def kernel(
    plan,
    right_leaf,
    inverse_leaf,
    lower_leaf,
    present,
    right_middle,
    inverse_middle,
    upper_middle,
    right_top,
    inverse_top,
    upper_top,
    solve_leaf,
    solve_middle,
    solve_top,
    *scratch,
):
    names = [name for name, _ in scratch_list(plan)]
    s = dict(zip(names, scratch))
    send, recv = s["send"], s["recv"]
    n, levels, block, chunk, width = plan.n, plan.levels, plan.block, plan.chunk, plan.width
    share = block // n
    nbits = len(plan.gbits)
    place = {axis: lax.axis_index(axis) for axis in AXES}
    me = place["gcol"]
    counter = [0]

    def bit_of(bit):
        return (place[bit[0]] // 2 ** bit[1]) % 2

    def partner(bit):
        return {bit[0]: place[bit[0]] + (1 - 2 * bit_of(bit)) * 2 ** bit[1]}

    def ship(source, target, where):
        slot = counter[0]
        counter[0] += 1
        copy = pltpu.make_async_remote_copy(
            src_ref=source,
            dst_ref=target,
            send_sem=send.at[slot],
            recv_sem=recv.at[slot],
            device_id=where,
            device_id_type=pl.DeviceIdType.MESH,
        )
        copy.start()
        return copy

    nx = n // 2
    core, row_x = me % 2, me // 2
    quarter_rows = share // 4
    mate, opposite, above = partner(("gcol", 0)), partner(("leaf", 0)), partner(("grow", 0))
    leaf_bit, grow_bit = bit_of(("leaf", 0)), bit_of(("grow", 0))
    tops = s["tops"]
    offsets = range(1, nx)

    barrier = pltpu.get_barrier_semaphore()
    far = [{"gcol": (row_x + d) % nx * 2 + core} for d in offsets]
    greeted = [partner(bit) for bit in plan.bits if bit[0] != "gcol" or bit[1] == 0] + far
    for device in greeted:
        pl.semaphore_signal(
            barrier, inc=1, device_id=device, device_id_type=pl.DeviceIdType.MESH
        )
    for level in range(levels):
        tops[level, me] = inverse_top[level].reshape(2, 2, quarter_rows, block)
    for pair in range(plan.mats - levels):
        tops[levels + pair, me] = upper_top[pair].reshape(2, 2, quarter_rows, block)
    pl.semaphore_wait(barrier, len(greeted))

    mats = range(plan.mats)
    across, over, up, mated = [], [], [], []

    def pieces():
        return [(m, (row_x - d + nx) % nx * 2 + core) for m in mats for d in offsets]

    def send_over():
        for (m, source), copy in zip(pieces(), across):
            copy.wait()
            piece = tops.at[m, source, grow_bit, leaf_bit]
            over.append(ship(piece, piece, opposite))

    def send_up():
        for (m, source), copy in zip(pieces(), over):
            copy.wait()
            piece = tops.at[m, source, grow_bit]
            up.append(ship(piece, piece, above))
            mated.append(ship(piece, piece, mate))

    def end_up():
        for (m, source), copy in zip(pieces(), up):
            copy.wait()
            piece = tops.at[m, source, 1 - grow_bit]
            mated.append(ship(piece, piece, mate))

    for m in mats:
        mine = tops.at[m, me, grow_bit, leaf_bit]
        across += [ship(mine, mine, device) for device in far]
    for m in mats:
        mated.append(ship(tops.at[m, me], tops.at[m, me], mate))
    done = set()

    def once(name, act):
        if name not in done:
            done.add(name)
            act()

    kept = present[0, 0, 0].astype(jnp.float32)
    leaf_fwd = mul(split(inverse_leaf[0, 0, 0]), split(right_leaf[0, 0, 0]))
    s["leaf_fwd"][...] = leaf_fwd
    lower_pair = split(lower_leaf[0, 0, 0])
    lead = ((place["leaf"] + place["grow"]) == 0).astype(jnp.float32)
    bits_shape = (2,) * len(plan.halved)

    def fill_inverse():
        high, low = split(inverse_leaf[0, 0, 0].T)
        s["inv_high"][...] = high
        s["inv_low"][...] = low

    def fill_lower():
        high, low = split(lower_leaf[0, 0, 0].T)
        s["low_high"][...] = high
        s["low_low"][...] = low

    def keep(name, pair, *where):
        for kind, value in zip(("high", "low"), pair):
            s[f"{name}_{kind}"][(*where, Ellipsis)] = value

    def kept_pair(name, *where):
        return tuple(s[f"{name}_{kind}"][(*where, Ellipsis)] for kind in ("high", "low"))

    def fill_middle():
        keep("im", split(inverse_middle[0, 0]))
        for level in range(levels):
            keep("um", split(upper_middle[level, 0, 0]), level)

    def fill_middle_turned():
        keep("imt", split(inverse_middle[0, 0].T))

    def split_tops():
        for m in range(plan.mats):
            high, low = split(tops[m].reshape(block, block))
            s["top_high"][m] = high
            s["top_low"][m] = low

    def finish_tops():
        end_up()
        for copy in mated:
            copy.wait()
        split_tops()

    def narrow(value, m, dims):
        rest = value - value.astype(jnp.bfloat16).astype(jnp.float32)
        both = jnp.concatenate([value, rest], axis=0).astype(jnp.bfloat16)
        high, low = s["top_high"][m], s["top_low"][m]

        def dot(a, b):
            return lax.dot_general(a, b, (dims, ((), ())), preferred_element_type=jnp.float32)

        wide = dot(both, high)
        return wide[:chunk] + (wide[chunk:] + dot(both, low)[:chunk])

    def index(known, bit=None, flip=False):
        where = []
        for b in plan.halved:
            if b in known:
                where.append(bit_of(b))
            elif b == bit:
                where.append(1 - bit_of(b) if flip else bit_of(b))
            else:
                where.append(slice(None))
        return tuple(where)

    def scatter_sum(blocks, landing):
        at = 0
        for t, bit in enumerate(plan.gbits):
            low = me % 2**t
            count = n >> (t + 1)
            theirs = low + (1 - bit_of(bit)) * 2**t
            mine = low + bit_of(bit) * 2**t
            copies = [
                ship(blocks.at[theirs + j * 2 ** (t + 1)], landing.at[at + j], partner(bit))
                for j in range(count)
            ]
            yield
            for j, copy in enumerate(copies):
                copy.wait()
                where = mine + j * 2 ** (t + 1)
                blocks[where] = blocks[where] + landing[at + j]
            at += count

    def gather(blocks):
        for t in reversed(range(nbits)):
            low = me % 2 ** (t + 1)
            copies = [
                ship(*(blocks.at[low + j * 2 ** (t + 1)],) * 2, partner(plan.gbits[t]))
                for j in range(n >> (t + 1))
            ]
            yield
            for copy in copies:
                copy.wait()

    def pipeline(p):
        cols = slice(p * width, (p + 1) * width)
        own = index(plan.halved)
        mid, mid_full = s["mid"].at[p], s["mid_full"].at[p]
        part = mul(lower_pair, split(s["leaf_fwd"][:, cols])) * kept
        mid[...] = part.reshape(n, share, width)
        for t, _ in enumerate(scatter_sum(mid, s["mid_land"].at[p])):
            if t == nbits - 1:
                once("middle", fill_middle)
                once("lower", fill_lower)
            yield
        mid_full[me] = right_middle[0, 0, :, cols] - mid[me]
        for t, _ in enumerate(gather(mid_full)):
            if t == 0:
                once("over", send_over)
                once("inverse", fill_inverse)
            yield
        once("up", send_up)
        middle_fwd = mul(kept_pair("im"), split(mid_full[...].reshape(block, width)))
        s["middle_fwd"][p] = middle_fwd

        fwd_turned = split(middle_fwd.T)
        for level in range(levels):
            turned = mul(fwd_turned, kept_pair("um", level))
            right = right_top[level, :, cols].T * lead
            placed = jnp.concatenate(
                [right * (me == c).astype(jnp.float32) for c in range(n)], axis=1
            )
            s[f"top{p}_{level}"][...] = (placed - turned).reshape(bits_shape + (chunk, block))
        for step in range(len(plan.halved)):
            copies = []
            for level in range(levels):
                order = plan.order(level)
                there = index(order[:step], order[step], True)
                copies.append(
                    ship(
                        s[f"top{p}_{level}"].at[there],
                        s[f"land{p}_{level}_{step}"],
                        partner(order[step]),
                    )
                )
            yield
            for level in range(levels):
                here = index(plan.order(level)[: step + 1])
                top = s[f"top{p}_{level}"]
                copies[level].wait()
                top[here] = top[here] + s[f"land{p}_{level}_{step}"][...]
        for step, bit in enumerate(plan.rest):
            copies = [
                ship(
                    s[f"top{p}_{level}"].at[own],
                    s[f"rest{p}"].at[step, level],
                    partner(bit),
                )
                for level in range(levels)
            ]
            once("tops", finish_tops)
            yield
            for level in range(levels):
                top = s[f"top{p}_{level}"]
                copies[level].wait()
                top[own] = top[own] + s[f"rest{p}"][step, level]

        once("tops", finish_tops)
        top_fwd = []
        for level in range(levels):
            residual = s[f"top{p}_{level}"][own]
            for lower in range(level):
                m = levels + pair_index(level, lower)
                residual = residual - narrow(top_fwd[lower], m, NN)
            top_fwd.append(narrow(residual, level, NT))
        top_back = [None] * levels
        for level in reversed(range(levels)):
            residual = top_fwd[level]
            for higher in range(level + 1, levels):
                m = levels + pair_index(higher, level)
                residual = residual - narrow(top_back[higher], m, NT)
            top_back[level] = narrow(residual, level, NN)
            s[f"back{p}_{level}"][own] = top_back[level]
        for step in reversed(range(len(plan.halved))):
            copies = []
            for level in range(levels):
                order = plan.order(level)
                held = s[f"back{p}_{level}"].at[index(order[: step + 1])]
                copies.append(ship(held, held, partner(order[step])))
            once("turned", fill_middle_turned)
            yield
            for copy in copies:
                copy.wait()

        residual = s["middle_fwd"][p]
        for level in range(levels):
            turned = s[f"back{p}_{level}"][...].reshape(width, block)
            residual = residual - mul(kept_pair("um", level), split(turned), NT)
        mid2, mid2_full = s["mid2"].at[p], s["mid2_full"].at[p]
        mid2[...] = mul(kept_pair("imt"), split(residual)).reshape(n, share, width)
        steps = scatter_sum(mid2, s["mid2_land"].at[p])
        next(steps)
        for level in range(levels):
            rows = s["top_rows"].at[level]
            rows[...] = s[f"back{p}_{level}"][...].reshape(width, block).T
            solve_top[level, :, cols] = rows[pl.ds(pl.multiple_of(me * share, share), share), :]
        yield
        yield from steps
        solve_middle[0, 0, :, cols] = mid2[me]
        mid2_full[me] = mid2[me]
        yield from gather(mid2_full)
        middle = split(mid2_full[...].reshape(block, width))
        leaf_res = s["leaf_fwd"][:, cols] - kept * mul(
            (s["low_high"][...], s["low_low"][...]), middle
        )
        solve_leaf[0, 0, 0, :, cols] = mul((s["inv_high"][...], s["inv_low"][...]), split(leaf_res))

    running = [pipeline(p) for p in range(plan.parts)]
    while running:
        running = [steps for steps in running if next(steps, StopIteration) is not StopIteration]


def scratch_list(plan):
    n, levels, block, width, chunk = plan.n, plan.levels, plan.block, plan.width, plan.chunk
    share, parts = block // n, plan.parts
    f32, b16 = jnp.float32, jnp.bfloat16
    nh, slots = len(plan.halved), plan.slots()
    out = [
        ("send", pltpu.SemaphoreType.DMA((slots,))),
        ("recv", pltpu.SemaphoreType.DMA((slots,))),
        ("leaf_fwd", pltpu.VMEM((block, plan.columns), f32)),
        ("inv_high", pltpu.VMEM((block, block), b16)),
        ("inv_low", pltpu.VMEM((block, block), b16)),
        ("low_high", pltpu.VMEM((block, block), b16)),
        ("low_low", pltpu.VMEM((block, block), b16)),
        ("im_high", pltpu.VMEM((share, block), b16)),
        ("im_low", pltpu.VMEM((share, block), b16)),
        ("imt_high", pltpu.VMEM((block, share), b16)),
        ("imt_low", pltpu.VMEM((block, share), b16)),
        ("um_high", pltpu.VMEM((levels, share, block), b16)),
        ("um_low", pltpu.VMEM((levels, share, block), b16)),
        ("mid", pltpu.VMEM((parts, n, share, width), f32)),
        ("mid_land", pltpu.VMEM((parts, n - 1, share, width), f32)),
        ("mid_full", pltpu.VMEM((parts, n, share, width), f32)),
        ("middle_fwd", pltpu.VMEM((parts, share, width), f32)),
        ("mid2", pltpu.VMEM((parts, n, share, width), f32)),
        ("mid2_full", pltpu.VMEM((parts, n, share, width), f32)),
        ("mid2_land", pltpu.VMEM((parts, n - 1, share, width), f32)),
        ("tops", pltpu.VMEM((plan.mats, n, 2, 2, share // 4, block), f32)),
        ("top_high", pltpu.VMEM((plan.mats, block, block), b16)),
        ("top_low", pltpu.VMEM((plan.mats, block, block), b16)),
        ("top_rows", pltpu.VMEM((levels, block, width), f32)),
    ]
    for p in range(parts):
        if plan.rest:
            out.append((f"rest{p}", pltpu.VMEM((len(plan.rest), levels, chunk, block), f32)))
        for level in range(levels):
            out.append((f"top{p}_{level}", pltpu.VMEM((2,) * nh + (chunk, block), f32)))
            out.append((f"back{p}_{level}", pltpu.VMEM((2,) * nh + (chunk, block), f32)))
            for step in range(nh):
                shape = (2,) * (nh - step - 1) + (chunk, block)
                out.append((f"land{p}_{level}_{step}", pltpu.VMEM(shape, f32)))
    return out


def copy_out(*refs):
    count = len(refs) // 2
    for source, target in zip(refs[:count], refs[count:]):
        target[...] = source[...]


def local(sizes, *args):
    right_leaf, right_middle, right_top = args[0], args[4], args[7]
    block, columns = right_leaf.shape[-2:]
    plan = Plan(sizes, right_top.shape[0], block, columns)
    vmem = pl.BlockSpec(memory_space=pltpu.VMEM)
    in_specs = [vmem] * len(args)
    in_specs[3] = pl.BlockSpec(memory_space=pltpu.SMEM)
    solved = pl.pallas_call(
        functools.partial(kernel, plan),
        out_shape=(
            jax.ShapeDtypeStruct(right_leaf.shape, jnp.float32),
            jax.ShapeDtypeStruct(right_middle.shape, jnp.float32),
            jax.ShapeDtypeStruct(right_top.shape, jnp.float32),
        ),
        in_specs=in_specs,
        out_specs=(vmem,) * 3,
        scratch_shapes=[shape for _, shape in scratch_list(plan)],
        compiler_params=pltpu.CompilerParams(
            collective_id=0, has_side_effects=True, vmem_limit_bytes=56 * 2**20
        ),
    )(*args)
    return pl.pallas_call(
        copy_out,
        out_shape=tuple(jax.ShapeDtypeStruct(x.shape, x.dtype) for x in solved),
        in_specs=[vmem] * len(solved),
        out_specs=(vmem,) * len(solved),
    )(*solved)


def solution(mesh):
    in_specs = (
        P("leaf", "grow", "gcol", None, None),
        P("leaf", "grow", "gcol", None, None),
        P("leaf", "grow", "gcol", None, None),
        P("leaf", "grow", "gcol"),
        P("leaf", "grow", "gcol", None),
        P("leaf", "grow", "gcol", None),
        P(None, "leaf", "grow", "gcol", None),
        P(None, "gcol", None),
        P(None, "gcol", None),
        P(None, "gcol", None),
    )
    out_specs = (
        P("leaf", "grow", "gcol", None, None),
        P("leaf", "grow", "gcol", None),
        P(None, "gcol", None),
    )
    sizes = {axis: mesh.shape[axis] for axis in AXES}
    return jax.shard_map(
        functools.partial(local, sizes),
        mesh=mesh,
        in_specs=in_specs,
        out_specs=out_specs,
        check_vma=False,
    )
```

```python
import functools

import jax
import jax.numpy as jnp
from jax import lax
from jax.experimental import pallas as pl
from jax.experimental.pallas import tpu as pltpu
from jax.sharding import PartitionSpec as P

PARTS = 2
AXES = ("gcol", "leaf", "grow")
NN = ((1,), (0,))
NT = ((1,), (1,))


def pair_index(upper_level, lower_level):
    return upper_level * (upper_level - 1) // 2 + lower_level


def split(value):
    high = value.astype(jnp.bfloat16)
    low = (value - high.astype(jnp.float32)).astype(jnp.bfloat16)
    return high, low


def mul(left, right, dims=NN):
    def dot(a, b):
        return lax.dot_general(a, b, (dims, ((), ())), preferred_element_type=jnp.float32)

    return dot(left[0], right[0]) + (dot(left[0], right[1]) + dot(left[1], right[0]))


class Plan:
    def __init__(self, sizes, levels, block, columns):
        self.sizes, self.levels, self.block = sizes, levels, block
        self.parts = PARTS
        self.columns, self.width = columns, columns // PARTS
        self.n = sizes["gcol"]
        self.gbits = [("gcol", t) for t in range(self.n.bit_length() - 1)]
        others = [(a, t) for a in AXES[1:] for t in range(sizes[a].bit_length() - 1)]
        self.bits = self.gbits + others
        count = 0
        while count < len(self.bits) and self.width >> (count + 1) >= 8:
            count += 1
        self.halved, self.rest = self.bits[:count], self.bits[count:]
        self.chunk = self.width >> count
        first = self.gbits[:1]
        self.orders = [
            self.halved,
            first
            + [b for b in self.halved if b[0] == "leaf"]
            + [b for b in self.halved if b[0] == "gcol" and b not in first]
            + [b for b in self.halved if b[0] == "grow"],
        ]
        self.mats = levels + levels * (levels - 1) // 2

    def order(self, level):
        return self.orders[level % 2]

    def slots(self):
        n, nx = self.n, self.n // 2
        middle = 4 * (n - 1)
        top = (2 * len(self.halved) + len(self.rest)) * self.levels
        spread = self.mats * (1 + 5 * (nx - 1))
        return self.parts * (middle + top) + spread


def kernel(
    plan,
    right_leaf,
    inverse_leaf,
    lower_leaf,
    present,
    right_middle,
    inverse_middle,
    upper_middle,
    right_top,
    inverse_top,
    upper_top,
    solve_leaf,
    solve_middle,
    solve_top,
    *scratch,
):
    names = [name for name, _ in scratch_list(plan)]
    s = dict(zip(names, scratch))
    send, recv = s["send"], s["recv"]
    n, levels, block, chunk, width = plan.n, plan.levels, plan.block, plan.chunk, plan.width
    share = block // n
    nbits = len(plan.gbits)
    place = {axis: lax.axis_index(axis) for axis in AXES}
    me = place["gcol"]
    counter = [0]

    def bit_of(bit):
        return (place[bit[0]] // 2 ** bit[1]) % 2

    def partner(bit):
        return {bit[0]: place[bit[0]] + (1 - 2 * bit_of(bit)) * 2 ** bit[1]}

    def ship(source, target, where):
        slot = counter[0]
        counter[0] += 1
        copy = pltpu.make_async_remote_copy(
            src_ref=source,
            dst_ref=target,
            send_sem=send.at[slot],
            recv_sem=recv.at[slot],
            device_id=where,
            device_id_type=pl.DeviceIdType.MESH,
        )
        copy.start()
        return copy

    nx = n // 2
    core, row_x = me % 2, me // 2
    quarter_rows = share // 4
    mate, opposite, above = partner(("gcol", 0)), partner(("leaf", 0)), partner(("grow", 0))
    leaf_bit, grow_bit = bit_of(("leaf", 0)), bit_of(("grow", 0))
    tops = s["tops"]
    offsets = range(1, nx)

    barrier = pltpu.get_barrier_semaphore()
    far = [{"gcol": (row_x + d) % nx * 2 + core} for d in offsets]
    greeted = [partner(bit) for bit in plan.bits if bit[0] != "gcol" or bit[1] == 0] + far
    for device in greeted:
        pl.semaphore_signal(
            barrier, inc=1, device_id=device, device_id_type=pl.DeviceIdType.MESH
        )
    for level in range(levels):
        tops[level, me] = inverse_top[level].reshape(2, 2, quarter_rows, block)
    for pair in range(plan.mats - levels):
        tops[levels + pair, me] = upper_top[pair].reshape(2, 2, quarter_rows, block)
    pl.semaphore_wait(barrier, len(greeted))

    mats = range(plan.mats)
    across, over, up, mated = [], [], [], []

    def pieces():
        return [(m, (row_x - d + nx) % nx * 2 + core) for m in mats for d in offsets]

    def send_over():
        for (m, source), copy in zip(pieces(), across):
            copy.wait()
            piece = tops.at[m, source, grow_bit, leaf_bit]
            over.append(ship(piece, piece, opposite))

    def send_up():
        for (m, source), copy in zip(pieces(), over):
            copy.wait()
            piece = tops.at[m, source, grow_bit]
            up.append(ship(piece, piece, above))
            mated.append(ship(piece, piece, mate))

    def end_up():
        for (m, source), copy in zip(pieces(), up):
            copy.wait()
            piece = tops.at[m, source, 1 - grow_bit]
            mated.append(ship(piece, piece, mate))

    for m in mats:
        mine = tops.at[m, me, grow_bit, leaf_bit]
        across += [ship(mine, mine, device) for device in far]
    for m in mats:
        mated.append(ship(tops.at[m, me], tops.at[m, me], mate))
    done = set()

    def once(name, act):
        if name not in done:
            done.add(name)
            act()

    kept = present[0, 0, 0].astype(jnp.float32)
    leaf_fwd = mul(split(inverse_leaf[0, 0, 0]), split(right_leaf[0, 0, 0]))
    s["leaf_fwd"][...] = leaf_fwd
    lower_pair = split(lower_leaf[0, 0, 0])
    lead = ((place["leaf"] + place["grow"]) == 0).astype(jnp.float32)
    bits_shape = (2,) * len(plan.halved)

    def fill_inverse():
        high, low = split(inverse_leaf[0, 0, 0].T)
        s["inv_high"][...] = high
        s["inv_low"][...] = low

    def fill_lower():
        high, low = split(lower_leaf[0, 0, 0].T)
        s["low_high"][...] = high
        s["low_low"][...] = low

    def keep(name, pair, *where):
        for kind, value in zip(("high", "low"), pair):
            s[f"{name}_{kind}"][(*where, Ellipsis)] = value

    def kept_pair(name, *where):
        return tuple(s[f"{name}_{kind}"][(*where, Ellipsis)] for kind in ("high", "low"))

    def fill_middle():
        keep("im", split(inverse_middle[0, 0]))
        for level in range(levels):
            keep("um", split(upper_middle[level, 0, 0]), level)

    def fill_middle_turned():
        keep("imt", split(inverse_middle[0, 0].T))

    def split_tops():
        for m in range(plan.mats):
            high, low = split(tops[m].reshape(block, block))
            s["top_high"][m] = high
            s["top_low"][m] = low

    def finish_tops():
        end_up()
        for copy in mated:
            copy.wait()
        split_tops()

    def narrow(value, m, dims):
        rows = value.shape[0]
        rest = value - value.astype(jnp.bfloat16).astype(jnp.float32)
        both = jnp.concatenate([value, rest], axis=0).astype(jnp.bfloat16)
        high, low = s["top_high"][m], s["top_low"][m]

        def dot(a, b):
            return lax.dot_general(a, b, (dims, ((), ())), preferred_element_type=jnp.float32)

        wide = dot(both, high)
        return wide[:rows] + (wide[rows:] + dot(both, low)[:rows])

    def index(known, bit=None, flip=False):
        where = []
        for b in plan.halved:
            if b in known:
                where.append(bit_of(b))
            elif b == bit:
                where.append(1 - bit_of(b) if flip else bit_of(b))
            else:
                where.append(slice(None))
        return tuple(where)

    def scatter_sum(blocks, landing):
        at = 0
        for t, bit in enumerate(plan.gbits):
            low = me % 2**t
            count = n >> (t + 1)
            theirs = low + (1 - bit_of(bit)) * 2**t
            mine = low + bit_of(bit) * 2**t
            copies = [
                ship(blocks.at[theirs + j * 2 ** (t + 1)], landing.at[at + j], partner(bit))
                for j in range(count)
            ]
            yield
            for j, copy in enumerate(copies):
                copy.wait()
                where = mine + j * 2 ** (t + 1)
                blocks[where] = blocks[where] + landing[at + j]
            at += count

    def gather(blocks):
        for t in reversed(range(nbits)):
            low = me % 2 ** (t + 1)
            copies = [
                ship(*(blocks.at[low + j * 2 ** (t + 1)],) * 2, partner(plan.gbits[t]))
                for j in range(n >> (t + 1))
            ]
            yield
            for copy in copies:
                copy.wait()

    own = index(plan.halved)

    def solve_tops():
        once("tops", finish_tops)
        top_fwd = []
        for level in range(levels):
            residual = jnp.concatenate(
                [s[f"top{p}_{level}"][own] for p in range(plan.parts)], axis=0
            )
            for lower in range(level):
                m = levels + pair_index(level, lower)
                residual = residual - narrow(top_fwd[lower], m, NN)
            top_fwd.append(narrow(residual, level, NT))
        top_back = [None] * levels
        for level in reversed(range(levels)):
            residual = top_fwd[level]
            for higher in range(level + 1, levels):
                m = levels + pair_index(higher, level)
                residual = residual - narrow(top_back[higher], m, NT)
            top_back[level] = narrow(residual, level, NN)
            for p in range(plan.parts):
                s[f"back{p}_{level}"][own] = top_back[level][p * chunk : (p + 1) * chunk]

    def pipeline(p):
        cols = slice(p * width, (p + 1) * width)
        last = p == plan.parts - 1
        mid, mid_full = s["mid"].at[p], s["mid_full"].at[p]
        part = mul(lower_pair, split(s["leaf_fwd"][:, cols])) * kept
        mid[...] = part.reshape(n, share, width)
        for t, _ in enumerate(scatter_sum(mid, s["mid_land"].at[p])):
            if t == nbits - 1 and last:
                fill_middle()
                fill_lower()
            yield
        mid_full[me] = right_middle[0, 0, :, cols] - mid[me]
        for t, _ in enumerate(gather(mid_full)):
            if t == 0:
                once("over", send_over)
                if last:
                    fill_inverse()
            yield
        once("up", send_up)
        middle_fwd = mul(kept_pair("im"), split(mid_full[...].reshape(block, width)))
        s["middle_fwd"][p] = middle_fwd

        fwd_turned = split(middle_fwd.T)
        for level in range(levels):
            turned = mul(fwd_turned, kept_pair("um", level))
            right = right_top[level, :, cols].T * lead
            placed = jnp.concatenate(
                [right * (me == c).astype(jnp.float32) for c in range(n)], axis=1
            )
            s[f"top{p}_{level}"][...] = (placed - turned).reshape(bits_shape + (chunk, block))
        for step in range(len(plan.halved)):
            copies = []
            for level in range(levels):
                order = plan.order(level)
                there = index(order[:step], order[step], True)
                copies.append(
                    ship(
                        s[f"top{p}_{level}"].at[there],
                        s[f"land{p}_{level}_{step}"],
                        partner(order[step]),
                    )
                )
            yield
            for level in range(levels):
                here = index(plan.order(level)[: step + 1])
                top = s[f"top{p}_{level}"]
                copies[level].wait()
                top[here] = top[here] + s[f"land{p}_{level}_{step}"][...]
        for step, bit in enumerate(plan.rest):
            copies = [
                ship(
                    s[f"top{p}_{level}"].at[own],
                    s[f"rest{p}"].at[step, level],
                    partner(bit),
                )
                for level in range(levels)
            ]
            if last:
                once("tops", finish_tops)
            yield
            for level in range(levels):
                top = s[f"top{p}_{level}"]
                copies[level].wait()
                top[own] = top[own] + s[f"rest{p}"][step, level]

        yield
        once("solve", solve_tops)
        for step in reversed(range(len(plan.halved))):
            copies = []
            for level in range(levels):
                order = plan.order(level)
                held = s[f"back{p}_{level}"].at[index(order[: step + 1])]
                copies.append(ship(held, held, partner(order[step])))
            if last:
                once("turned", fill_middle_turned)
            yield
            for copy in copies:
                copy.wait()

        residual = s["middle_fwd"][p]
        for level in range(levels):
            turned = s[f"back{p}_{level}"][...].reshape(width, block)
            residual = residual - mul(kept_pair("um", level), split(turned), NT)
        mid2, mid2_full = s["mid2"].at[p], s["mid2_full"].at[p]
        mid2[...] = mul(kept_pair("imt"), split(residual)).reshape(n, share, width)
        yield from scatter_sum(mid2, s["mid2_land"].at[p])
        mid2_full[me] = mid2[me]
        steps = gather(mid2_full)
        next(steps)
        solve_middle[0, 0, :, cols] = mid2[me]
        for level in range(levels):
            rows = s["top_rows"].at[level]
            rows[...] = s[f"back{p}_{level}"][...].reshape(width, block).T
            solve_top[level, :, cols] = rows[pl.ds(pl.multiple_of(me * share, share), share), :]
        yield
        yield from steps
        middle = split(mid2_full[...].reshape(block, width))
        leaf_res = s["leaf_fwd"][:, cols] - kept * mul(
            (s["low_high"][...], s["low_low"][...]), middle
        )
        solve_leaf[0, 0, 0, :, cols] = mul((s["inv_high"][...], s["inv_low"][...]), split(leaf_res))

    running = [pipeline(p) for p in range(plan.parts)]
    while running:
        running = [steps for steps in running if next(steps, StopIteration) is not StopIteration]


def scratch_list(plan):
    n, levels, block, width, chunk = plan.n, plan.levels, plan.block, plan.width, plan.chunk
    share, parts = block // n, plan.parts
    f32, b16 = jnp.float32, jnp.bfloat16
    nh, slots = len(plan.halved), plan.slots()
    out = [
        ("send", pltpu.SemaphoreType.DMA((slots,))),
        ("recv", pltpu.SemaphoreType.DMA((slots,))),
        ("leaf_fwd", pltpu.VMEM((block, plan.columns), f32)),
        ("inv_high", pltpu.VMEM((block, block), b16)),
        ("inv_low", pltpu.VMEM((block, block), b16)),
        ("low_high", pltpu.VMEM((block, block), b16)),
        ("low_low", pltpu.VMEM((block, block), b16)),
        ("im_high", pltpu.VMEM((share, block), b16)),
        ("im_low", pltpu.VMEM((share, block), b16)),
        ("imt_high", pltpu.VMEM((block, share), b16)),
        ("imt_low", pltpu.VMEM((block, share), b16)),
        ("um_high", pltpu.VMEM((levels, share, block), b16)),
        ("um_low", pltpu.VMEM((levels, share, block), b16)),
        ("mid", pltpu.VMEM((parts, n, share, width), f32)),
        ("mid_land", pltpu.VMEM((parts, n - 1, share, width), f32)),
        ("mid_full", pltpu.VMEM((parts, n, share, width), f32)),
        ("middle_fwd", pltpu.VMEM((parts, share, width), f32)),
        ("mid2", pltpu.VMEM((parts, n, share, width), f32)),
        ("mid2_full", pltpu.VMEM((parts, n, share, width), f32)),
        ("mid2_land", pltpu.VMEM((parts, n - 1, share, width), f32)),
        ("tops", pltpu.VMEM((plan.mats, n, 2, 2, share // 4, block), f32)),
        ("top_high", pltpu.VMEM((plan.mats, block, block), b16)),
        ("top_low", pltpu.VMEM((plan.mats, block, block), b16)),
        ("top_rows", pltpu.VMEM((levels, block, width), f32)),
    ]
    for p in range(parts):
        if plan.rest:
            out.append((f"rest{p}", pltpu.VMEM((len(plan.rest), levels, chunk, block), f32)))
        for level in range(levels):
            out.append((f"top{p}_{level}", pltpu.VMEM((2,) * nh + (chunk, block), f32)))
            out.append((f"back{p}_{level}", pltpu.VMEM((2,) * nh + (chunk, block), f32)))
            for step in range(nh):
                shape = (2,) * (nh - step - 1) + (chunk, block)
                out.append((f"land{p}_{level}_{step}", pltpu.VMEM(shape, f32)))
    return out


def copy_out(*refs):
    count = len(refs) // 2
    for source, target in zip(refs[:count], refs[count:]):
        target[...] = source[...]


def local(sizes, *args):
    right_leaf, right_middle, right_top = args[0], args[4], args[7]
    block, columns = right_leaf.shape[-2:]
    plan = Plan(sizes, right_top.shape[0], block, columns)
    vmem = pl.BlockSpec(memory_space=pltpu.VMEM)
    in_specs = [vmem] * len(args)
    in_specs[3] = pl.BlockSpec(memory_space=pltpu.SMEM)
    solved = pl.pallas_call(
        functools.partial(kernel, plan),
        out_shape=(
            jax.ShapeDtypeStruct(right_leaf.shape, jnp.float32),
            jax.ShapeDtypeStruct(right_middle.shape, jnp.float32),
            jax.ShapeDtypeStruct(right_top.shape, jnp.float32),
        ),
        in_specs=in_specs,
        out_specs=(vmem,) * 3,
        scratch_shapes=[shape for _, shape in scratch_list(plan)],
        compiler_params=pltpu.CompilerParams(
            collective_id=0, has_side_effects=True, vmem_limit_bytes=56 * 2**20
        ),
    )(*args)
    return pl.pallas_call(
        copy_out,
        out_shape=tuple(jax.ShapeDtypeStruct(x.shape, x.dtype) for x in solved),
        in_specs=[vmem] * len(solved),
        out_specs=(vmem,) * len(solved),
    )(*solved)


def solution(mesh):
    in_specs = (
        P("leaf", "grow", "gcol", None, None),
        P("leaf", "grow", "gcol", None, None),
        P("leaf", "grow", "gcol", None, None),
        P("leaf", "grow", "gcol"),
        P("leaf", "grow", "gcol", None),
        P("leaf", "grow", "gcol", None),
        P(None, "leaf", "grow", "gcol", None),
        P(None, "gcol", None),
        P(None, "gcol", None),
        P(None, "gcol", None),
    )
    out_specs = (
        P("leaf", "grow", "gcol", None, None),
        P("leaf", "grow", "gcol", None),
        P(None, "gcol", None),
    )
    sizes = {axis: mesh.shape[axis] for axis in AXES}
    return jax.shard_map(
        functools.partial(local, sizes),
        mesh=mesh,
        in_specs=in_specs,
        out_specs=out_specs,
        check_vma=False,
    )
```
